32 devices in a mesh: groups: 2 (over y), fsdp: 4 (over z), sub: 2 (over x), pair: 2 (over core).
Axes of the slice: x: 2, y: 2, z: 4, core: 2. Of those that a mesh axis runs over, the one named last changes fastest.
Arguments:
- gradient: float32 [6, 1024, 1024], P('groups', ('fsdp', 'pair'), 'sub'), parts along dimension 0, may hold values from -6 to 6
- owner_table: int32 [6], P('groups'), parts along dimension 0, may hold values from 0 to 3, as said below
- left_basis: bfloat16 [8, 2, 4, 2, 128, 1024], P(('groups', 'fsdp'), None, None, 'pair'), parts along dimension 0, may hold values from -0.1875 to 0.1875
- right_basis: bfloat16 [8, 2, 1024, 1024], P(('groups', 'fsdp'), None, 'sub'), parts along dimension 0, may hold values from -0.1875 to 0.1875
- first_moment: float32 [8, 1024, 2, 1024], P(('groups', 'fsdp'), 'pair', None, 'sub'), parts along dimension 0, may hold values from -3 to 3
- second_moment: float32 [8, 1024, 2, 1024], P(('groups', 'fsdp'), 'pair', None, 'sub'), parts along dimension 0, may hold values from 0.02 to 1
Outputs:
- update: float32 [6, 1024, 1024], P('groups', ('fsdp', 'pair'), 'sub'), parts along dimension 0
- new_first: float32 [8, 1024, 2, 1024], P(('groups', 'fsdp'), 'pair', None, 'sub'), parts along dimension 0
- new_second: float32 [8, 1024, 2, 1024], P(('groups', 'fsdp'), 'pair', None, 'sub'), parts along dimension 0
The draws below stay inside these ranges and needn't reach their ends.
There are 2 independent parts, one for each index of `groups`. The reference program is written for one: setup_inputs(seed, part) draws one part's arguments, and reference() takes and returns one part's arrays. A program takes and returns all parts, laid end to end along the dimension named above; each array names one. Nothing has to cross between parts.
Inputs may be any that keep to these rules, and one draw needn't show every extreme that they name: `owner_table`: no owner is named by more than 2 blocks, and one owner by exactly 2.
All inputs are finite; a program needn't handle non-finite values.
Results may differ from the reference program's by a relative error of at most 0.012.
Values may be sent and summed in bfloat16 or wider, within the bound.
A program may use at most 64 MiB of HBM per device.

```python
import math
import jax
import jax.numpy as jnp
from jax import lax

BS = 1024
MAXB = 2
STEP = 10
NB = 3
N_FSDP = 4
N_SUB = 2
N_PAIR = 2


def draw_owner_table(key, part):
    key = jax.random.fold_in(key, 11)
    key_first, key_second, key_third = jax.random.split(key, 3)
    chosen = jax.random.randint(key_first, (), 0, N_FSDP).astype(jnp.int32)
    others = ((jnp.arange(N_FSDP - 1, dtype=jnp.int32) + chosen + 1) % N_FSDP).astype(jnp.int32)
    slot_ids = jax.random.permutation(key_second, (N_FSDP - 1) * MAXB)[:NB - MAXB]
    remaining = others[slot_ids // MAXB]
    owners_all = jnp.concatenate([jnp.full((MAXB,), 0, jnp.int32) + chosen, remaining.astype(jnp.int32)])
    order = jax.random.permutation(key_third, NB)
    return owners_all[order].astype(jnp.int32)


def level_of(rng, shape, shards, low, high):
    factor_of = 1.0
    for dim, shards_of in shards:
        heights = jax.random.uniform(jax.random.fold_in(jax.random.fold_in(rng, 6), dim), (shards_of,), jnp.float32, low / len(shards), high / len(shards))
        factor_of = factor_of * jnp.repeat(jnp.exp(heights), shape[dim] // shards_of).reshape((-1,) + (1,) * (len(shape) - 1 - dim))
    return factor_of


def bell_draw(rng, shape, deviation, most, cuts=(), kind=jnp.bfloat16):
    values = deviation * jax.random.normal(rng, shape, jnp.float32)
    if cuts:
        values = values * level_of(rng, shape, cuts, -0.22, 0.18)
    return jnp.clip(values, -most, most).astype(kind)


def setup_inputs(seed: int = 0, part: int = 0) -> dict:
    arg_keys = jax.random.split(jax.random.key(seed), 7)
    own_keys = jax.random.split(jax.random.fold_in(arg_keys[6], part), 7)
    gradient = bell_draw(own_keys[0], (NB, BS, BS), 1.0, 6.0, ((1, 8), (2, 2)), jnp.float32)
    owner_table = draw_owner_table(jax.random.fold_in(jax.random.fold_in(arg_keys[6], part), 71), part)
    left_basis = bell_draw(own_keys[2], (N_FSDP, MAXB, N_FSDP, N_PAIR, BS // (N_FSDP * N_PAIR), BS), BS ** -0.5, 0.1875, ((0, 4), (3, 2)))
    right_basis = bell_draw(own_keys[3], (N_FSDP, MAXB, BS, BS), BS ** -0.5, 0.1875, ((0, 4), (2, 2)))
    first_moment = bell_draw(own_keys[4], (N_FSDP, BS, MAXB, BS), 0.3, 3.0, ((0, 4), (1, 2), (3, 2)), jnp.float32)
    second_moment = jnp.clip(jnp.exp(math.log(1.0) - 3.912023 * jax.random.uniform(own_keys[5], (N_FSDP, BS, MAXB, BS), jnp.float32) ** level_of(own_keys[5], (N_FSDP, BS, MAXB, BS), ((0, 4), (1, 2), (3, 2)), -0.2, 0.2)), 0.02, 1.0)
    return dict(gradient=gradient, owner_table=owner_table, left_basis=left_basis, right_basis=right_basis, first_moment=first_moment, second_moment=second_moment)


BETA_ONE = 0.95
BETA_TWO = 0.95
EPSILON = 1e-08

def slot_tables(owner_table):
    assigned = (owner_table[:, None] == jnp.arange(N_FSDP, dtype=jnp.int32)[None, :]).astype(jnp.int32)
    before = jnp.cumsum(assigned, axis=0) - assigned
    slot_rank = lax.optimization_barrier(jnp.sum(before * assigned, axis=1)).astype(jnp.int32)
    placed = assigned[:, None, :] * (slot_rank[:, None, None] == jnp.arange(MAXB, dtype=jnp.int32)[None, :, None]).astype(jnp.int32)
    source = lax.optimization_barrier(jnp.sum(placed * jnp.arange(NB, dtype=jnp.int32)[:, None, None], axis=0)).astype(jnp.int32)
    filled = lax.optimization_barrier(jnp.sum(placed, axis=0))
    return (slot_rank, source, filled)

def reference(gradient, owner_table, left_basis, right_basis, first_moment, second_moment):
    slot_rank, source, filled = slot_tables(owner_table)
    left_full = left_basis.reshape(N_FSDP, MAXB, BS, BS)
    col_share = BS // N_SUB
    corr_one = 1.0 - BETA_ONE ** STEP
    corr_two = 1.0 - BETA_TWO ** STEP

    def one_slot(slot_id):
        owner = slot_id // MAXB
        within = slot_id % MAXB
        block_id = source[within, owner]
        grad_half = gradient[block_id].astype(jnp.bfloat16)
        left_mat = left_full[owner, within]
        right_mat = right_basis[owner, within]
        grad_groups = grad_half.astype(jnp.float32).reshape(BS, N_SUB, col_share)
        right_groups = right_mat.astype(jnp.float32).reshape(N_SUB, col_share, BS)
        partials = jnp.einsum('isk,skj->sij', grad_groups, right_groups).astype(jnp.bfloat16)
        rotated_right = lax.optimization_barrier(jnp.sum(partials.astype(jnp.float32), axis=0)).astype(jnp.bfloat16)
        rotated = jnp.dot(left_mat.T, rotated_right, preferred_element_type=jnp.float32)
        moment_one = first_moment[owner, :, within, :]
        moment_two = second_moment[owner, :, within, :]
        next_one = BETA_ONE * moment_one + (1.0 - BETA_ONE) * rotated
        next_two = BETA_TWO * moment_two + (1.0 - BETA_TWO) * rotated * rotated
        normed = (next_one / corr_one / (jnp.sqrt(next_two / corr_two) + EPSILON)).astype(jnp.bfloat16)
        back_rot = jnp.dot(normed, right_mat.T, preferred_element_type=jnp.float32).astype(jnp.bfloat16)
        step_block = jnp.dot(left_mat, back_rot, preferred_element_type=jnp.float32)
        keep_slot = filled[within, owner] > 0
        return (step_block, jnp.where(keep_slot, next_one, moment_one), jnp.where(keep_slot, next_two, moment_two))
    steps_all, ones_all, twos_all = lax.map(one_slot, jnp.arange(N_FSDP * MAXB, dtype=jnp.int32))
    steps_all = steps_all.reshape(N_FSDP, MAXB, BS, BS)
    new_first = jnp.transpose(ones_all.reshape(N_FSDP, MAXB, BS, BS), (0, 2, 1, 3))
    new_second = jnp.transpose(twos_all.reshape(N_FSDP, MAXB, BS, BS), (0, 2, 1, 3))
    update = steps_all[owner_table, slot_rank]
    return (update, new_first, new_second)
```

```python
import functools

import jax
import jax.numpy as jnp
from jax import lax
from jax.experimental import pallas as pl
from jax.experimental.pallas import tpu as pltpu
from jax.sharding import PartitionSpec as P

STEP = 10


BETA_ONE = 0.95
BETA_TWO = 0.95
EPSILON = 1e-08

MESH = pl.DeviceIdType.MESH
BF = jnp.bfloat16
F32 = jnp.float32


def send(src, dst, send_sem, recv_sem, where):
    return pltpu.make_async_remote_copy(
        src_ref=src,
        dst_ref=dst,
        send_sem=send_sem,
        recv_sem=recv_sem,
        device_id=where,
        device_id_type=MESH,
    )


def kernel(
    owners,
    subs,
    table,
    grad,
    left_hbm,
    right_hbm,
    one_hbm,
    two_hbm,
    update,
    one_out,
    two_out,
    left,
    left_t,
    right,
    one,
    two,
    one_new,
    two_new,
    grad_send,
    grad_recv,
    part_send,
    part_recv,
    part_own,
    rot_send,
    rot_recv,
    rot_own,
    normed,
    back,
    step_send,
    step_recv,
    load_sem,
    store_sem,
    gs_sem,
    gr_sem,
    ps_sem,
    pr_sem,
    rs_sem,
    rr_sem,
    ns_sem,
    nr_sem,
    bs_sem,
    br_sem,
    us_sem,
    ur_sem,
):
    blocks, shard, share = grad.shape
    slots, half, order = left.shape
    tile = min(256, share)
    z = lax.axis_index("fsdp")
    x = lax.axis_index("sub")
    c = lax.axis_index("pair")
    z_peers = [lax.rem(z + d, owners) for d in range(1, owners)]
    x_peers = [lax.rem(x + d, subs) for d in range(1, subs)]

    loads = [
        pltpu.make_async_copy(src, dst, load_sem.at[n])
        for n, (src, dst) in enumerate(
            ((right_hbm, right), (left_hbm, left), (one_hbm, one), (two_hbm, two))
        )
    ]
    for load in loads:
        load.start()

    barrier = pltpu.get_barrier_semaphore()
    for o in z_peers:
        pl.semaphore_signal(barrier, inc=1, device_id={"fsdp": o}, device_id_type=MESH)
    for s in x_peers:
        pl.semaphore_signal(barrier, inc=1, device_id={"sub": s}, device_id_type=MESH)
    pl.semaphore_signal(barrier, inc=1, device_id={"pair": 1 - c}, device_id_type=MESH)

    owner = [table[b] for b in range(blocks)]
    rank = []
    for b in range(blocks):
        r = jnp.int32(0)
        for e in range(b):
            r = r + jnp.where(owner[e] == owner[b], 1, 0)
        rank.append(r)

    def source(o, k):
        n = jnp.int32(0)
        for b in range(blocks):
            n = n + jnp.where((owner[b] == o) & (rank[b] == k), b, 0)
        return n

    count = jnp.int32(0)
    for b in range(blocks):
        count = count + jnp.where(owner[b] == z, 1, 0)

    pending = []
    for k in range(slots):
        for d, o in enumerate(z_peers):
            grad_send[k, d] = grad[source(o, k)].astype(BF)
            if k == 0 and d == 0:
                pl.semaphore_wait(barrier, len(z_peers) + len(x_peers) + 1)
            copy = send(
                grad_send.at[k, d],
                grad_recv.at[k, z],
                gs_sem.at[k, d],
                gr_sem.at[k, z],
                {"fsdp": o},
            )
            copy.start()
            pending.append(copy)
        grad_recv[k, z] = grad[source(z, k)].astype(BF)

    loads[0].wait()
    loads[1].wait()
    for k in range(slots):
        for n in range(0, half, tile):
            left_t[k, :, n : n + tile] = left[k, n : n + tile, :].T

    def wait_from(buffer, sems, k, peers, axis):
        for p in peers:
            send(buffer.at[k, p], buffer.at[k, p], sems.at[k, p], sems.at[k, p], {axis: p}).wait_recv()

    def columns(s, n):
        return pl.ds(pl.multiple_of(s * share + n, tile), tile)

    def rotate_right(k):
        wait_from(grad_recv, gr_sem, k, z_peers, "fsdp")
        g = grad_recv[k].reshape(half, share)
        for d, s in enumerate(x_peers):
            for n in range(0, share, tile):
                part_send[k, d, :, n : n + tile] = jnp.dot(
                    g, right[k, :, columns(s, n)], preferred_element_type=F32
                ).astype(BF)
            copy = send(
                part_send.at[k, d],
                part_recv.at[k, x],
                ps_sem.at[k, d],
                pr_sem.at[k, x],
                {"sub": s},
            )
            copy.start()
            pending.append(copy)
        for n in range(0, share, tile):
            part_own[k, :, n : n + tile] = jnp.dot(
                g, right[k, :, columns(x, n)], preferred_element_type=F32
            ).astype(BF)

    def rotate_left(k):
        wait_from(part_recv, pr_sem, k, x_peers, "sub")
        for n in range(0, share, tile):
            cols = slice(n, n + tile)
            total = part_own[k, :, cols].astype(F32)
            for s in x_peers:
                total = total + part_recv[k, s, :, cols].astype(F32)
            part_own[k, :, cols] = total.astype(BF)
        other = pl.ds(pl.multiple_of((1 - c) * half, half), half)
        mine = pl.ds(pl.multiple_of(c * half, half), half)
        for n in range(0, share, tile):
            cols = slice(n, n + tile)
            rot_send[k, :, cols] = jnp.dot(
                left_t[k, other, :], part_own[k, :, cols], preferred_element_type=F32
            ).astype(BF)
        copy = send(rot_send.at[k], rot_recv.at[k], rs_sem.at[k], rr_sem.at[k], {"pair": 1 - c})
        copy.start()
        pending.append(copy)
        for n in range(0, share, tile):
            cols = slice(n, n + tile)
            rot_own[:, cols] = jnp.dot(
                left_t[k, mine, :], part_own[k, :, cols], preferred_element_type=F32
            )
        copy.wait_recv()

    corr_one = 1.0 - BETA_ONE**STEP
    corr_two = 1.0 - BETA_TWO**STEP

    def moments(k):
        used = count > k
        rows = 32

        @pl.loop(0, half // rows)
        def _(i):
            at = pl.ds(pl.multiple_of(i * rows, rows), rows)
            r = rot_own[at, :] + rot_recv[k, at, :].astype(F32)
            m_old = one[at, k, :]
            v_old = two[at, k, :]
            m = BETA_ONE * m_old + (1.0 - BETA_ONE) * r
            v = BETA_TWO * v_old + (1.0 - BETA_TWO) * r * r
            one_new[at, k, :] = jnp.where(used, m, m_old)
            two_new[at, k, :] = jnp.where(used, v, v_old)
            normed[k, x, at, :] = (
                m / corr_one / (jnp.sqrt(v / corr_two) + EPSILON)
            ).astype(BF)

        for d, s in enumerate(x_peers):
            copy = send(
                normed.at[k, x],
                normed.at[k, x],
                ns_sem.at[k, d],
                nr_sem.at[k, x],
                {"sub": s},
            )
            copy.start()
            pending.append(copy)

    def back_rotate(k):
        wait_from(normed, nr_sem, k, x_peers, "sub")
        for n in range(0, share, tile):
            total = jnp.zeros((half, tile), F32)
            for s in range(subs):
                total = total + lax.dot_general(
                    normed[k, s],
                    right[k, n : n + tile, s * share : (s + 1) * share],
                    (((1,), (1,)), ((), ())),
                    preferred_element_type=F32,
                )
            back[k, c, :, n : n + tile] = total.astype(BF)
        copy = send(back.at[k, c], back.at[k, c], bs_sem.at[k], br_sem.at[k], {"pair": 1 - c})
        copy.start()
        pending.append(copy)
        send(
            back.at[k, 1 - c], back.at[k, 1 - c], bs_sem.at[k], br_sem.at[k], {"pair": 1 - c}
        ).wait_recv()
        b = back[k].reshape(order, share)
        for n in range(0, share, tile):
            rows = jnp.dot(left[k], b[:, n : n + tile], preferred_element_type=F32).astype(BF)
            step_send[k, :, :, n : n + tile] = rows.reshape(owners, shard, tile)
        for d, o in enumerate(z_peers):
            copy = send(
                step_send.at[k, o],
                step_recv.at[k, z],
                us_sem.at[k, d],
                ur_sem.at[k, z],
                {"fsdp": o},
            )
            copy.start()
            pending.append(copy)
        step_recv[k, z] = step_send[k, z]

    rotate_right(0)
    rotate_right(1)
    rotate_left(0)
    loads[2].wait()
    loads[3].wait()
    moments(0)
    rotate_left(1)
    moments(1)
    stores = [
        pltpu.make_async_copy(one_new, one_out, store_sem.at[0]),
        pltpu.make_async_copy(two_new, two_out, store_sem.at[1]),
    ]
    for store in stores:
        store.start()
    back_rotate(0)
    back_rotate(1)
    for k in range(slots):
        wait_from(step_recv, ur_sem, k, z_peers, "fsdp")
    for b in range(blocks):
        update[b] = step_recv[jnp.minimum(rank[b], slots - 1), owner[b]].astype(F32)
    for copy in pending:
        copy.wait_send()
    for store in stores:
        store.wait()


def shards(
    owners, subs, gradient, owner_table, left_basis, right_basis, first_moment, second_moment
):
    slots, order = right_basis.shape[1], right_basis.shape[3]
    blocks, shard, share = gradient.shape
    half = owners * shard
    left_rows = left_basis.reshape(slots, half, order)
    right_rows = right_basis.reshape(slots, share, order)
    one = first_moment.reshape(half, slots, share)
    two = second_moment.reshape(half, slots, share)
    dma = pltpu.SemaphoreType.DMA
    whole = pl.BlockSpec(memory_space=pl.ANY)
    vmem = pl.BlockSpec(memory_space=pltpu.VMEM)
    moment = jax.ShapeDtypeStruct((half, slots, share), F32)
    update, new_one, new_two = pl.pallas_call(
        functools.partial(kernel, owners, subs),
        out_shape=(jax.ShapeDtypeStruct((blocks, shard, share), F32), moment, moment),
        in_specs=[pl.BlockSpec(memory_space=pltpu.SMEM), vmem, whole, whole, whole, whole],
        out_specs=(vmem, whole, whole),
        scratch_shapes=[
            pltpu.VMEM((slots, half, order), BF),
            pltpu.VMEM((slots, order, half), BF),
            pltpu.VMEM((slots, share, order), BF),
            pltpu.VMEM((half, slots, share), F32),
            pltpu.VMEM((half, slots, share), F32),
            pltpu.VMEM((half, slots, share), F32),
            pltpu.VMEM((half, slots, share), F32),
            pltpu.VMEM((slots, owners - 1, shard, share), BF),
            pltpu.VMEM((slots, owners, shard, share), BF),
            pltpu.VMEM((slots, subs - 1, half, share), BF),
            pltpu.VMEM((slots, subs, half, share), BF),
            pltpu.VMEM((slots, half, share), BF),
            pltpu.VMEM((slots, half, share), BF),
            pltpu.VMEM((slots, half, share), BF),
            pltpu.VMEM((half, share), F32),
            pltpu.VMEM((slots, subs, half, share), BF),
            pltpu.VMEM((slots, 2, half, share), BF),
            pltpu.VMEM((slots, owners, shard, share), BF),
            pltpu.VMEM((slots, owners, shard, share), BF),
            dma((4,)),
            dma((2,)),
            dma((slots, owners)),
            dma((slots, owners)),
            dma((slots, subs)),
            dma((slots, subs)),
            dma((slots,)),
            dma((slots,)),
            dma((slots, subs)),
            dma((slots, subs)),
            dma((slots,)),
            dma((slots,)),
            dma((slots, owners)),
            dma((slots, owners)),
        ],
        compiler_params=pltpu.CompilerParams(
            collective_id=0, has_side_effects=True, vmem_limit_bytes=48 * 2**20
        ),
        cost_estimate=pl.CostEstimate(
            flops=10 * slots * half * order * share,
            bytes_accessed=20 * slots * half * share,
            transcendentals=slots * half * share,
        ),
    )(owner_table, gradient, left_rows, right_rows, one, two)
    return (update, new_one[None], new_two[None])


def solution(mesh):
    return jax.shard_map(
        functools.partial(shards, mesh.shape["fsdp"], mesh.shape["sub"]),
        mesh=mesh,
        in_specs=(
            P("groups", ("fsdp", "pair"), "sub"),
            P("groups"),
            P(("groups", "fsdp"), None, None, "pair", None, None),
            P(("groups", "fsdp"), None, "sub", None),
            P(("groups", "fsdp"), "pair", None, "sub"),
            P(("groups", "fsdp"), "pair", None, "sub"),
        ),
        out_specs=(
            P("groups", ("fsdp", "pair"), "sub"),
            P(("groups", "fsdp"), "pair", None, "sub"),
            P(("groups", "fsdp"), "pair", None, "sub"),
        ),
        check_vma=False,
    )
```

```python
import functools

import jax
import jax.numpy as jnp
from jax import lax
from jax.experimental import pallas as pl
from jax.experimental.pallas import tpu as pltpu
from jax.sharding import PartitionSpec as P

STEP = 10


BETA_ONE = 0.95
BETA_TWO = 0.95
EPSILON = 1e-08

MESH = pl.DeviceIdType.MESH
BF = jnp.bfloat16
F32 = jnp.float32


def send(src, dst, send_sem, recv_sem, where):
    return pltpu.make_async_remote_copy(
        src_ref=src,
        dst_ref=dst,
        send_sem=send_sem,
        recv_sem=recv_sem,
        device_id=where,
        device_id_type=MESH,
    )


def kernel(
    owners,
    subs,
    table,
    grad,
    left_hbm,
    right_hbm,
    one_hbm,
    two_hbm,
    update,
    one_out,
    two_out,
    left,
    left_t,
    right,
    one,
    two,
    one_new,
    two_new,
    grad_own,
    grad_far,
    grad_send,
    grad_recv,
    late_send,
    late_recv,
    far_send,
    far,
    part_send,
    part_recv,
    part_own,
    rot_send,
    rot_recv,
    rot_own,
    normed,
    back_sum,
    back,
    step_send,
    step_recv,
    load_sem,
    store_sem,
    gs_sem,
    gr_sem,
    as_sem,
    ar_sem,
    ls_sem,
    lr_sem,
    fs_sem,
    fr_sem,
    hs_sem,
    hr_sem,
    ps_sem,
    pr_sem,
    rs_sem,
    rr_sem,
    ns_sem,
    nr_sem,
    bs_sem,
    br_sem,
    us_sem,
    ur_sem,
):
    blocks, shard, share = grad.shape
    slots, half, order = left.shape
    tile = min(256, share)
    z = lax.axis_index("fsdp")
    x = lax.axis_index("sub")
    c = lax.axis_index("pair")
    z_peers = [lax.rem(z + d, owners) for d in range(1, owners)]
    x_peers = [lax.rem(x + d, subs) for d in range(1, subs)]

    loads = [
        pltpu.make_async_copy(src, dst, load_sem.at[n])
        for n, (src, dst) in enumerate(
            ((right_hbm, right), (left_hbm, left), (one_hbm, one), (two_hbm, two))
        )
    ]
    for load in loads:
        load.start()

    barrier = pltpu.get_barrier_semaphore()
    for o in z_peers:
        pl.semaphore_signal(barrier, inc=1, device_id={"fsdp": o}, device_id_type=MESH)
    for s in x_peers:
        pl.semaphore_signal(barrier, inc=1, device_id={"sub": s}, device_id_type=MESH)
    pl.semaphore_signal(barrier, inc=1, device_id={"pair": 1 - c}, device_id_type=MESH)

    owner = [table[b] for b in range(blocks)]
    rank = []
    for b in range(blocks):
        r = jnp.int32(0)
        for e in range(b):
            r = r + jnp.where(owner[e] == owner[b], 1, 0)
        rank.append(r)

    def source(o, k):
        n = jnp.int32(0)
        for b in range(blocks):
            n = n + jnp.where((owner[b] == o) & (rank[b] == k), b, 0)
        return n

    count = jnp.int32(0)
    for b in range(blocks):
        count = count + jnp.where(owner[b] == z, 1, 0)

    last = slots - 1
    chunks = share // tile
    part = share // 2
    other = pl.ds(pl.multiple_of((1 - c) * half, half), half)
    mine = pl.ds(pl.multiple_of(c * half, half), half)
    pending = []

    def go(src, dst, send_sem, recv_sem, where):
        copy = send(src, dst, send_sem, recv_sem, where)
        copy.start()
        pending.append(copy)
        return copy

    def arrive(ref, sem, where):
        send(ref, ref, sem, sem, where).wait_recv()

    grad_own[...] = grad[...].astype(BF)
    pl.semaphore_wait(barrier, len(z_peers) + len(x_peers) + 1)
    early = []
    for k in range(last):
        for d, o in enumerate(z_peers):
            grad_send[k, d] = grad_own[source(o, k)]
            copy = send(
                grad_send.at[k, d], grad_recv.at[k, z], gs_sem.at[k, d], gr_sem.at[k, z], {"fsdp": o}
            )
            copy.start()
            early.append(copy)
        grad_recv[k, z] = grad_own[source(z, k)]
    for d, s in enumerate(x_peers):
        go(grad_own, grad_far.at[x], as_sem.at[d], ar_sem.at[x], {"sub": s})

    def columns(s, n):
        return pl.ds(pl.multiple_of(s * share + n, tile), tile)

    def columns_of(s):
        return pl.ds(pl.multiple_of(s * share, share), share)

    loads[0].wait()
    for d, s in enumerate(x_peers):
        far_send[d] = right[last, pl.ds(pl.multiple_of(c * part, part), part), columns_of(s)]
        go(far_send.at[d], far.at[x, c], fs_sem.at[d], fr_sem.at[x], {"sub": s})

    loads[1].wait()
    for k in range(slots):
        for n in range(0, half, tile):
            left_t[k, :, n : n + tile] = left[k, n : n + tile, :].T

    for copy in early:
        copy.wait_send()
    for n, s in enumerate([x] + x_peers):
        if n == 1:
            for p in x_peers:
                arrive(grad_far.at[p], ar_sem.at[p], {"sub": p})
        rows = (lambda i: grad_far[s, i]) if n else (lambda i: grad_own[i])
        for d, o in enumerate(z_peers):
            late_send[n, d] = rows(source(o, last))
            go(
                late_send.at[n, d],
                late_recv.at[n, z],
                ls_sem.at[n, d],
                lr_sem.at[n, z],
                {"fsdp": o},
            )
        late_recv[n, z] = rows(source(z, last))
    for d, s in enumerate(x_peers):
        arrive(far.at[s, c], fr_sem.at[s], {"sub": s})
        go(far.at[s, c], far.at[s, c], hs_sem.at[d], hr_sem.at[d], {"pair": 1 - c})

    def rotate_right(k):
        for p in z_peers:
            arrive(grad_recv.at[k, p], gr_sem.at[k, p], {"fsdp": p})
        g = grad_recv[k].reshape(half, share)
        for ch in range(chunks):
            for d, s in enumerate(x_peers):
                part_send[k, d, ch] = jnp.dot(
                    g, right[k, :, columns(s, ch * tile)], preferred_element_type=F32
                ).astype(BF)
                go(
                    part_send.at[k, d, ch],
                    part_recv.at[k, x, ch],
                    ps_sem.at[k, d, ch],
                    pr_sem.at[k, x, ch],
                    {"sub": s},
                )
        for ch in range(chunks):
            part_own[k, ch] = jnp.dot(
                g, right[k, :, columns(x, ch * tile)], preferred_element_type=F32
            ).astype(BF)

    def collect(k, ch):
        total = part_own[k, ch].astype(F32)
        for s in x_peers:
            arrive(part_recv.at[k, s, ch], pr_sem.at[k, s, ch], {"sub": s})
            total = total + part_recv[k, s, ch].astype(F32)
        part_own[k, ch] = total.astype(BF)

    def rotate_right_last():
        for n in range(subs):
            for p in z_peers:
                arrive(late_recv.at[n, p], lr_sem.at[n, p], {"fsdp": p})
        for d, s in enumerate(x_peers):
            arrive(far.at[s, 1 - c], hr_sem.at[d], {"pair": 1 - c})
        for ch in range(chunks):
            total = jnp.dot(
                late_recv[0].reshape(half, share),
                right[last, :, columns(x, ch * tile)],
                preferred_element_type=F32,
            )
            for n, s in enumerate(x_peers):
                total = total + jnp.dot(
                    late_recv[n + 1].reshape(half, share),
                    far[s].reshape(share, share)[:, ch * tile : (ch + 1) * tile],
                    preferred_element_type=F32,
                )
            part_own[last, ch] = total.astype(BF)

    def rotate_left(k, ch):
        rot_send[k, ch] = jnp.dot(
            left_t[k, other, :], part_own[k, ch], preferred_element_type=F32
        ).astype(BF)
        go(
            rot_send.at[k, ch],
            rot_recv.at[k, ch],
            rs_sem.at[k, ch],
            rr_sem.at[k, ch],
            {"pair": 1 - c},
        )
        rot_own[...] = jnp.dot(left_t[k, mine, :], part_own[k, ch], preferred_element_type=F32)
        arrive(rot_recv.at[k, ch], rr_sem.at[k, ch], {"pair": 1 - c})

    corr_one = 1.0 - BETA_ONE**STEP
    corr_two = 1.0 - BETA_TWO**STEP

    def moments(k, ch):
        used = count > k
        rows = 64
        cols = slice(ch * tile, (ch + 1) * tile)

        @pl.loop(0, half // rows)
        def _(i):
            at = pl.ds(pl.multiple_of(i * rows, rows), rows)
            r = rot_own[at, :] + rot_recv[k, ch, at, :].astype(F32)
            m_old = one[at, k, cols]
            v_old = two[at, k, cols]
            m = BETA_ONE * m_old + (1.0 - BETA_ONE) * r
            v = BETA_TWO * v_old + (1.0 - BETA_TWO) * r * r
            one_new[at, k, cols] = jnp.where(used, m, m_old)
            two_new[at, k, cols] = jnp.where(used, v, v_old)
            normed[k, x, ch, at, :] = (
                m / corr_one / (jnp.sqrt(v / corr_two) + EPSILON)
            ).astype(BF)

        for d, s in enumerate(x_peers):
            go(
                normed.at[k, x, ch],
                normed.at[k, x, ch],
                ns_sem.at[k, d, ch],
                nr_sem.at[k, x, ch],
                {"sub": s},
            )

    def back_term(k, s, ch, n):
        return lax.dot_general(
            normed[k, s, ch],
            right[k, n * tile : (n + 1) * tile, columns(s, ch * tile)],
            (((1,), (1,)), ((), ())),
            preferred_element_type=F32,
        )

    def back_own(k):
        for n in range(chunks):
            total = back_term(k, x, 0, n)
            for ch in range(1, chunks):
                total = total + back_term(k, x, ch, n)
            back_sum[k, n] = total

    def back_rotate(k):
        for ch in range(chunks):
            for s in x_peers:
                arrive(normed.at[k, s, ch], nr_sem.at[k, s, ch], {"sub": s})
            for n in range(chunks):
                total = back_sum[k, n]
                for s in x_peers:
                    total = total + back_term(k, s, ch, n)
                if ch < chunks - 1:
                    back_sum[k, n] = total
                    continue
                back[k, n, c] = total.astype(BF)
                go(
                    back.at[k, n, c],
                    back.at[k, n, c],
                    bs_sem.at[k, n],
                    br_sem.at[k, n],
                    {"pair": 1 - c},
                )
        for n in range(chunks):
            arrive(back.at[k, n, 1 - c], br_sem.at[k, n], {"pair": 1 - c})
            step_send[k, n] = (
                jnp.dot(left[k], back[k, n].reshape(order, tile), preferred_element_type=F32)
                .astype(BF)
                .reshape(owners, shard, tile)
            )
            for d, o in enumerate(z_peers):
                go(
                    step_send.at[k, n, o],
                    step_recv.at[k, n, z],
                    us_sem.at[k, n, d],
                    ur_sem.at[k, n, z],
                    {"fsdp": o},
                )
            step_recv[k, n, z] = step_send[k, n, z]

    for k in range(last):
        rotate_right(k)
    loads[2].wait()
    loads[3].wait()
    for k in range(last):
        for ch in range(chunks):
            collect(k, ch)
            rotate_left(k, ch)
            moments(k, ch)
        back_own(k)
    rotate_right_last()
    for ch in range(chunks):
        rotate_left(last, ch)
        moments(last, ch)
    stores = [
        pltpu.make_async_copy(one_new, one_out, store_sem.at[0]),
        pltpu.make_async_copy(two_new, two_out, store_sem.at[1]),
    ]
    for store in stores:
        store.start()
    for k in range(last):
        back_rotate(k)
    back_own(last)
    back_rotate(last)
    for k in range(slots):
        for n in range(chunks):
            for p in z_peers:
                arrive(step_recv.at[k, n, p], ur_sem.at[k, n, p], {"fsdp": p})
    for n in range(chunks):
        for b in range(blocks):
            update[b, :, n * tile : (n + 1) * tile] = step_recv[
                jnp.minimum(rank[b], last), n, owner[b]
            ].astype(F32)
    for copy in pending:
        copy.wait_send()
    for store in stores:
        store.wait()


def shards(
    owners, subs, gradient, owner_table, left_basis, right_basis, first_moment, second_moment
):
    slots, order = right_basis.shape[1], right_basis.shape[3]
    blocks, shard, share = gradient.shape
    half = owners * shard
    left_rows = left_basis.reshape(slots, half, order)
    right_rows = right_basis.reshape(slots, share, order)
    one = first_moment.reshape(half, slots, share)
    two = second_moment.reshape(half, slots, share)
    tile = min(256, share)
    chunks = share // tile
    dma = pltpu.SemaphoreType.DMA
    whole = pl.BlockSpec(memory_space=pl.ANY)
    vmem = pl.BlockSpec(memory_space=pltpu.VMEM)
    moment = jax.ShapeDtypeStruct((half, slots, share), F32)
    update, new_one, new_two = pl.pallas_call(
        functools.partial(kernel, owners, subs),
        out_shape=(jax.ShapeDtypeStruct((blocks, shard, share), F32), moment, moment),
        in_specs=[pl.BlockSpec(memory_space=pltpu.SMEM), vmem, whole, whole, whole, whole],
        out_specs=(vmem, whole, whole),
        scratch_shapes=[
            pltpu.VMEM((slots, half, order), BF),
            pltpu.VMEM((slots, order, half), BF),
            pltpu.VMEM((slots, share, order), BF),
            pltpu.VMEM((half, slots, share), F32),
            pltpu.VMEM((half, slots, share), F32),
            pltpu.VMEM((half, slots, share), F32),
            pltpu.VMEM((half, slots, share), F32),
            pltpu.VMEM((blocks, shard, share), BF),
            pltpu.VMEM((subs, blocks, shard, share), BF),
            pltpu.VMEM((slots - 1, owners - 1, shard, share), BF),
            pltpu.VMEM((slots - 1, owners, shard, share), BF),
            pltpu.VMEM((subs, owners - 1, shard, share), BF),
            pltpu.VMEM((subs, owners, shard, share), BF),
            pltpu.VMEM((subs - 1, share // 2, share), BF),
            pltpu.VMEM((subs, 2, share // 2, share), BF),
            pltpu.VMEM((slots - 1, subs - 1, chunks, half, tile), BF),
            pltpu.VMEM((slots - 1, subs, chunks, half, tile), BF),
            pltpu.VMEM((slots, chunks, half, tile), BF),
            pltpu.VMEM((slots, chunks, half, tile), BF),
            pltpu.VMEM((slots, chunks, half, tile), BF),
            pltpu.VMEM((half, tile), F32),
            pltpu.VMEM((slots, subs, chunks, half, tile), BF),
            pltpu.VMEM((slots, chunks, half, tile), F32),
            pltpu.VMEM((slots, chunks, 2, half, tile), BF),
            pltpu.VMEM((slots, chunks, owners, shard, tile), BF),
            pltpu.VMEM((slots, chunks, owners, shard, tile), BF),
            dma((4,)),
            dma((2,)),
            dma((slots, owners)),
            dma((slots, owners)),
            dma((subs,)),
            dma((subs,)),
            dma((subs, owners)),
            dma((subs, owners)),
            dma((subs,)),
            dma((subs,)),
            dma((subs,)),
            dma((subs,)),
            dma((slots, subs, chunks)),
            dma((slots, subs, chunks)),
            dma((slots, chunks)),
            dma((slots, chunks)),
            dma((slots, subs, chunks)),
            dma((slots, subs, chunks)),
            dma((slots, chunks)),
            dma((slots, chunks)),
            dma((slots, chunks, owners)),
            dma((slots, chunks, owners)),
        ],
        compiler_params=pltpu.CompilerParams(
            collective_id=0, has_side_effects=True, vmem_limit_bytes=48 * 2**20
        ),
        cost_estimate=pl.CostEstimate(
            flops=10 * slots * half * order * share,
            bytes_accessed=20 * slots * half * share,
            transcendentals=slots * half * share,
        ),
    )(owner_table, gradient, left_rows, right_rows, one, two)
    return (update, new_one[None], new_two[None])


def solution(mesh):
    return jax.shard_map(
        functools.partial(shards, mesh.shape["fsdp"], mesh.shape["sub"]),
        mesh=mesh,
        in_specs=(
            P("groups", ("fsdp", "pair"), "sub"),
            P("groups"),
            P(("groups", "fsdp"), None, None, "pair", None, None),
            P(("groups", "fsdp"), None, "sub", None),
            P(("groups", "fsdp"), "pair", None, "sub"),
            P(("groups", "fsdp"), "pair", None, "sub"),
        ),
        out_specs=(
            P("groups", ("fsdp", "pair"), "sub"),
            P(("groups", "fsdp"), "pair", None, "sub"),
            P(("groups", "fsdp"), "pair", None, "sub"),
        ),
        check_vma=False,
    )
```

```python
import functools

import jax
import jax.numpy as jnp
from jax import lax
from jax.experimental import pallas as pl
from jax.experimental.pallas import tpu as pltpu
from jax.sharding import PartitionSpec as P

STEP = 10


BETA_ONE = 0.95
BETA_TWO = 0.95
EPSILON = 1e-08

MESH = pl.DeviceIdType.MESH
BF = jnp.bfloat16
F32 = jnp.float32


def send(src, dst, send_sem, recv_sem, where):
    return pltpu.make_async_remote_copy(
        src_ref=src,
        dst_ref=dst,
        send_sem=send_sem,
        recv_sem=recv_sem,
        device_id=where,
        device_id_type=MESH,
    )


def kernel(
    owners,
    subs,
    table,
    grad,
    left_hbm,
    right_hbm,
    one_hbm,
    two_hbm,
    update,
    one_out,
    two_out,
    left,
    left_t,
    right,
    one,
    two,
    one_new,
    two_new,
    grad_own,
    grad_far,
    grad_send,
    grad_recv,
    late_send,
    late_recv,
    far_send,
    far,
    part_send,
    part_recv,
    part_own,
    rot_send,
    rot_recv,
    rot_own,
    normed,
    back_sum,
    back,
    step_send,
    step_recv,
    load_sem,
    store_sem,
    gs_sem,
    gr_sem,
    as_sem,
    ar_sem,
    ls_sem,
    lr_sem,
    cs_sem,
    fs_sem,
    fr_sem,
    hs_sem,
    hr_sem,
    ps_sem,
    pr_sem,
    rs_sem,
    rr_sem,
    ns_sem,
    nr_sem,
    bs_sem,
    br_sem,
    us_sem,
    ur_sem,
):
    blocks, shard, share = grad.shape
    slots, half, order = left.shape
    tile = min(256, share)
    z = lax.axis_index("fsdp")
    x = lax.axis_index("sub")
    c = lax.axis_index("pair")
    z_peers = [lax.rem(z + d, owners) for d in range(1, owners)]
    x_peers = [lax.rem(x + d, subs) for d in range(1, subs)]

    loads = [
        pltpu.make_async_copy(src, dst, load_sem.at[n])
        for n, (src, dst) in enumerate(
            ((right_hbm, right), (left_hbm, left), (one_hbm, one), (two_hbm, two))
        )
    ]
    for load in loads:
        load.start()

    barrier = pltpu.get_barrier_semaphore()
    for o in z_peers:
        pl.semaphore_signal(barrier, inc=1, device_id={"fsdp": o}, device_id_type=MESH)
    for s in x_peers:
        pl.semaphore_signal(barrier, inc=1, device_id={"sub": s}, device_id_type=MESH)
    pl.semaphore_signal(barrier, inc=1, device_id={"pair": 1 - c}, device_id_type=MESH)

    owner = [table[b] for b in range(blocks)]
    rank = []
    for b in range(blocks):
        r = jnp.int32(0)
        for e in range(b):
            r = r + jnp.where(owner[e] == owner[b], 1, 0)
        rank.append(r)

    def source(o, k):
        n = jnp.int32(0)
        for b in range(blocks):
            n = n + jnp.where((owner[b] == o) & (rank[b] == k), b, 0)
        return n

    count = jnp.int32(0)
    for b in range(blocks):
        count = count + jnp.where(owner[b] == z, 1, 0)

    last = slots - 1
    chunks = share // tile
    part = share // 2
    other = pl.ds(pl.multiple_of((1 - c) * half, half), half)
    mine = pl.ds(pl.multiple_of(c * half, half), half)
    pending = []

    def go(src, dst, send_sem, recv_sem, where):
        copy = send(src, dst, send_sem, recv_sem, where)
        copy.start()
        pending.append(copy)
        return copy

    def arrive(ref, sem, where):
        send(ref, ref, sem, sem, where).wait_recv()

    grad_own[...] = grad[...].astype(BF)
    pl.semaphore_wait(barrier, len(z_peers) + len(x_peers) + 1)
    early = []
    for k in range(last):
        for d, o in enumerate(z_peers):
            grad_send[k, d] = grad_own[source(o, k)]
            copy = send(
                grad_send.at[k, d], grad_recv.at[k, z], gs_sem.at[k, d], gr_sem.at[k, z], {"fsdp": o}
            )
            copy.start()
            early.append(copy)
        grad_recv[k, z] = grad_own[source(z, k)]
    single = blocks < 2 * slots

    def travel(t, way):
        origin, after = z - way * t, z + way
        here = (origin >= 0) & (origin < owners)
        further = here & (after >= 0) & (after < owners)
        return here, further, jnp.clip(origin, 0, owners - 1), jnp.clip(after, 0, owners - 1)

    def chain(n, t, way, origin, after):
        return send(
            late_recv.at[n, origin],
            late_recv.at[n, origin],
            cs_sem.at[n, t, (1 - way) // 2],
            lr_sem.at[n, origin],
            {"fsdp": after},
        )

    def hop(n, t):
        for way in (1, -1):
            here, further, origin, after = travel(t, way)
            if t > 0:

                @pl.when(here)
                def _():
                    arrive(late_recv.at[n, origin], lr_sem.at[n, origin], {"fsdp": origin})

            if t < owners - 1:

                @pl.when(further)
                def _():
                    chain(n, t, way, origin, after).start()

    if single:
        only = jnp.int32(0)
        for b in range(blocks):
            only = only + jnp.where(rank[b] == last, b, 0)
        late_recv[0, z] = grad_own[jnp.minimum(only, blocks - 1)]
        for d, s in enumerate(x_peers):
            n = subs - 1 - d
            go(late_recv.at[0, z], late_recv.at[n, z], as_sem.at[d], ar_sem.at[n], {"sub": s})
        hop(0, 0)
    else:
        for d, s in enumerate(x_peers):
            go(grad_own, grad_far.at[x], as_sem.at[d], ar_sem.at[x], {"sub": s})

    def columns(s, n):
        return pl.ds(pl.multiple_of(s * share + n, tile), tile)

    def columns_of(s):
        return pl.ds(pl.multiple_of(s * share, share), share)

    loads[0].wait()
    for d, s in enumerate(x_peers):
        far_send[d] = right[last, pl.ds(pl.multiple_of(c * part, part), part), columns_of(s)]
        go(far_send.at[d], far.at[x, c], fs_sem.at[d], fr_sem.at[x], {"sub": s})

    loads[1].wait()
    for k in range(slots):
        for n in range(0, half, tile):
            left_t[k, :, n : n + tile] = left[k, n : n + tile, :].T

    if single:
        for n in range(1, subs):
            arrive(late_recv.at[n, z], ar_sem.at[n], {"sub": x_peers[n - 1]})
            hop(n, 0)
    else:
        for n, s in enumerate([x] + x_peers):
            if n == 1:
                for p in x_peers:
                    arrive(grad_far.at[p], ar_sem.at[p], {"sub": p})
            rows = (lambda i: grad_far[s, i]) if n else (lambda i: grad_own[i])
            for d, o in enumerate(z_peers):
                late_send[n, d] = rows(source(o, last))
                go(
                    late_send.at[n, d],
                    late_recv.at[n, z],
                    ls_sem.at[n, d],
                    lr_sem.at[n, z],
                    {"fsdp": o},
                )
            late_recv[n, z] = rows(source(z, last))
    for d, s in enumerate(x_peers):
        arrive(far.at[s, c], fr_sem.at[s], {"sub": s})
        go(far.at[s, c], far.at[s, c], hs_sem.at[d], hr_sem.at[d], {"pair": 1 - c})
    if single and owners > 2:
        for n in range(subs):
            hop(n, 1)

    def rotate_right(k):
        for p in z_peers:
            arrive(grad_recv.at[k, p], gr_sem.at[k, p], {"fsdp": p})
        g = grad_recv[k].reshape(half, share)
        for ch in range(chunks):
            for d, s in enumerate(x_peers):
                part_send[k, d, ch] = jnp.dot(
                    g, right[k, :, columns(s, ch * tile)], preferred_element_type=F32
                ).astype(BF)
                go(
                    part_send.at[k, d, ch],
                    part_recv.at[k, x, ch],
                    ps_sem.at[k, d, ch],
                    pr_sem.at[k, x, ch],
                    {"sub": s},
                )
        for ch in range(chunks):
            part_own[k, ch] = jnp.dot(
                g, right[k, :, columns(x, ch * tile)], preferred_element_type=F32
            ).astype(BF)

    def collect(k, ch):
        total = part_own[k, ch].astype(F32)
        for s in x_peers:
            arrive(part_recv.at[k, s, ch], pr_sem.at[k, s, ch], {"sub": s})
            total = total + part_recv[k, s, ch].astype(F32)
        part_own[k, ch] = total.astype(BF)

    def rotate_right_last():
        for n in range(subs):
            if single:
                hop(n, owners - 1)
                continue
            for p in z_peers:
                arrive(late_recv.at[n, p], lr_sem.at[n, p], {"fsdp": p})
        for d, s in enumerate(x_peers):
            arrive(far.at[s, 1 - c], hr_sem.at[d], {"pair": 1 - c})
        for ch in range(chunks):
            total = jnp.dot(
                late_recv[0].reshape(half, share),
                right[last, :, columns(x, ch * tile)],
                preferred_element_type=F32,
            )
            for n, s in enumerate(x_peers):
                total = total + jnp.dot(
                    late_recv[n + 1].reshape(half, share),
                    far[s].reshape(share, share)[:, ch * tile : (ch + 1) * tile],
                    preferred_element_type=F32,
                )
            part_own[last, ch] = total.astype(BF)

    def rotate_left(k, ch):
        rot_send[k, ch] = jnp.dot(
            left_t[k, other, :], part_own[k, ch], preferred_element_type=F32
        ).astype(BF)
        go(
            rot_send.at[k, ch],
            rot_recv.at[k, ch],
            rs_sem.at[k, ch],
            rr_sem.at[k, ch],
            {"pair": 1 - c},
        )
        rot_own[...] = jnp.dot(left_t[k, mine, :], part_own[k, ch], preferred_element_type=F32)
        arrive(rot_recv.at[k, ch], rr_sem.at[k, ch], {"pair": 1 - c})

    corr_one = 1.0 - BETA_ONE**STEP
    corr_two = 1.0 - BETA_TWO**STEP

    def moments(k, ch):
        used = count > k
        rows = 64
        cols = slice(ch * tile, (ch + 1) * tile)

        @pl.loop(0, half // rows)
        def _(i):
            at = pl.ds(pl.multiple_of(i * rows, rows), rows)
            r = rot_own[at, :] + rot_recv[k, ch, at, :].astype(F32)
            m_old = one[at, k, cols]
            v_old = two[at, k, cols]
            m = BETA_ONE * m_old + (1.0 - BETA_ONE) * r
            v = BETA_TWO * v_old + (1.0 - BETA_TWO) * r * r
            one_new[at, k, cols] = jnp.where(used, m, m_old)
            two_new[at, k, cols] = jnp.where(used, v, v_old)
            normed[k, x, ch, at, :] = (
                m / corr_one / (jnp.sqrt(v / corr_two) + EPSILON)
            ).astype(BF)

        for d, s in enumerate(x_peers):
            go(
                normed.at[k, x, ch],
                normed.at[k, x, ch],
                ns_sem.at[k, d, ch],
                nr_sem.at[k, x, ch],
                {"sub": s},
            )

    def back_term(k, s, ch, n):
        return lax.dot_general(
            normed[k, s, ch],
            right[k, n * tile : (n + 1) * tile, columns(s, ch * tile)],
            (((1,), (1,)), ((), ())),
            preferred_element_type=F32,
        )

    def back_own(k):
        for n in range(chunks):
            total = back_term(k, x, 0, n)
            for ch in range(1, chunks):
                total = total + back_term(k, x, ch, n)
            back_sum[k, n] = total

    def back_rotate(k):
        for ch in range(chunks):
            for s in x_peers:
                arrive(normed.at[k, s, ch], nr_sem.at[k, s, ch], {"sub": s})
            for n in range(chunks):
                total = back_sum[k, n]
                for s in x_peers:
                    total = total + back_term(k, s, ch, n)
                if ch < chunks - 1:
                    back_sum[k, n] = total
                    continue
                back[k, n, c] = total.astype(BF)
                go(
                    back.at[k, n, c],
                    back.at[k, n, c],
                    bs_sem.at[k, n],
                    br_sem.at[k, n],
                    {"pair": 1 - c},
                )
        for n in range(chunks):
            arrive(back.at[k, n, 1 - c], br_sem.at[k, n], {"pair": 1 - c})
            step_send[k, n] = (
                jnp.dot(left[k], back[k, n].reshape(order, tile), preferred_element_type=F32)
                .astype(BF)
                .reshape(owners, shard, tile)
            )
            for d, o in enumerate(z_peers):
                go(
                    step_send.at[k, n, o],
                    step_recv.at[k, n, z],
                    us_sem.at[k, n, d],
                    ur_sem.at[k, n, z],
                    {"fsdp": o},
                )
            step_recv[k, n, z] = step_send[k, n, z]

    for k in range(last):
        rotate_right(k)
    if single:
        for t in range(2, owners - 1):
            for n in range(subs):
                hop(n, t)
    loads[2].wait()
    loads[3].wait()
    for k in range(last):
        for ch in range(chunks):
            collect(k, ch)
            rotate_left(k, ch)
            moments(k, ch)
        back_own(k)
    rotate_right_last()
    for ch in range(chunks):
        rotate_left(last, ch)
        moments(last, ch)
    stores = [
        pltpu.make_async_copy(one_new, one_out, store_sem.at[0]),
        pltpu.make_async_copy(two_new, two_out, store_sem.at[1]),
    ]
    for store in stores:
        store.start()
    for k in range(last):
        back_rotate(k)
    back_own(last)
    back_rotate(last)
    for k in range(slots):
        for n in range(chunks):
            for p in z_peers:
                arrive(step_recv.at[k, n, p], ur_sem.at[k, n, p], {"fsdp": p})
    for n in range(chunks):
        for b in range(blocks):
            update[b, :, n * tile : (n + 1) * tile] = step_recv[
                jnp.minimum(rank[b], last), n, owner[b]
            ].astype(F32)
    for copy in early + pending:
        copy.wait_send()
    if single:
        for n in range(subs):
            for t in range(owners - 1):
                for way in (1, -1):
                    _, further, origin, after = travel(t, way)

                    @pl.when(further)
                    def _():
                        chain(n, t, way, origin, after).wait_send()

    for store in stores:
        store.wait()


def shards(
    owners, subs, gradient, owner_table, left_basis, right_basis, first_moment, second_moment
):
    slots, order = right_basis.shape[1], right_basis.shape[3]
    blocks, shard, share = gradient.shape
    half = owners * shard
    left_rows = left_basis.reshape(slots, half, order)
    right_rows = right_basis.reshape(slots, share, order)
    one = first_moment.reshape(half, slots, share)
    two = second_moment.reshape(half, slots, share)
    tile = min(256, share)
    chunks = share // tile
    dma = pltpu.SemaphoreType.DMA
    whole = pl.BlockSpec(memory_space=pl.ANY)
    vmem = pl.BlockSpec(memory_space=pltpu.VMEM)
    moment = jax.ShapeDtypeStruct((half, slots, share), F32)
    update, new_one, new_two = pl.pallas_call(
        functools.partial(kernel, owners, subs),
        out_shape=(jax.ShapeDtypeStruct((blocks, shard, share), F32), moment, moment),
        in_specs=[pl.BlockSpec(memory_space=pltpu.SMEM), vmem, whole, whole, whole, whole],
        out_specs=(vmem, whole, whole),
        scratch_shapes=[
            pltpu.VMEM((slots, half, order), BF),
            pltpu.VMEM((slots, order, half), BF),
            pltpu.VMEM((slots, share, order), BF),
            pltpu.VMEM((half, slots, share), F32),
            pltpu.VMEM((half, slots, share), F32),
            pltpu.VMEM((half, slots, share), F32),
            pltpu.VMEM((half, slots, share), F32),
            pltpu.VMEM((blocks, shard, share), BF),
            pltpu.VMEM((subs, blocks, shard, share), BF),
            pltpu.VMEM((slots - 1, owners - 1, shard, share), BF),
            pltpu.VMEM((slots - 1, owners, shard, share), BF),
            pltpu.VMEM((subs, owners - 1, shard, share), BF),
            pltpu.VMEM((subs, owners, shard, share), BF),
            pltpu.VMEM((subs - 1, share // 2, share), BF),
            pltpu.VMEM((subs, 2, share // 2, share), BF),
            pltpu.VMEM((slots - 1, subs - 1, chunks, half, tile), BF),
            pltpu.VMEM((slots - 1, subs, chunks, half, tile), BF),
            pltpu.VMEM((slots, chunks, half, tile), BF),
            pltpu.VMEM((slots, chunks, half, tile), BF),
            pltpu.VMEM((slots, chunks, half, tile), BF),
            pltpu.VMEM((half, tile), F32),
            pltpu.VMEM((slots, subs, chunks, half, tile), BF),
            pltpu.VMEM((slots, chunks, half, tile), F32),
            pltpu.VMEM((slots, chunks, 2, half, tile), BF),
            pltpu.VMEM((slots, chunks, owners, shard, tile), BF),
            pltpu.VMEM((slots, chunks, owners, shard, tile), BF),
            dma((4,)),
            dma((2,)),
            dma((slots, owners)),
            dma((slots, owners)),
            dma((subs,)),
            dma((subs,)),
            dma((subs, owners)),
            dma((subs, owners)),
            dma((subs, owners, 2)),
            dma((subs,)),
            dma((subs,)),
            dma((subs,)),
            dma((subs,)),
            dma((slots, subs, chunks)),
            dma((slots, subs, chunks)),
            dma((slots, chunks)),
            dma((slots, chunks)),
            dma((slots, subs, chunks)),
            dma((slots, subs, chunks)),
            dma((slots, chunks)),
            dma((slots, chunks)),
            dma((slots, chunks, owners)),
            dma((slots, chunks, owners)),
        ],
        compiler_params=pltpu.CompilerParams(
            collective_id=0, has_side_effects=True, vmem_limit_bytes=48 * 2**20
        ),
        cost_estimate=pl.CostEstimate(
            flops=10 * slots * half * order * share,
            bytes_accessed=20 * slots * half * share,
            transcendentals=slots * half * share,
        ),
    )(owner_table, gradient, left_rows, right_rows, one, two)
    return (update, new_one[None], new_two[None])


def solution(mesh):
    return jax.shard_map(
        functools.partial(shards, mesh.shape["fsdp"], mesh.shape["sub"]),
        mesh=mesh,
        in_specs=(
            P("groups", ("fsdp", "pair"), "sub"),
            P("groups"),
            P(("groups", "fsdp"), None, None, "pair", None, None),
            P(("groups", "fsdp"), None, "sub", None),
            P(("groups", "fsdp"), "pair", None, "sub"),
            P(("groups", "fsdp"), "pair", None, "sub"),
        ),
        out_specs=(
            P("groups", ("fsdp", "pair"), "sub"),
            P(("groups", "fsdp"), "pair", None, "sub"),
            P(("groups", "fsdp"), "pair", None, "sub"),
        ),
        check_vma=False,
    )
```

```python
import functools

import jax
import jax.numpy as jnp
from jax import lax
from jax.experimental import pallas as pl
from jax.experimental.pallas import tpu as pltpu
from jax.sharding import PartitionSpec as P

STEP = 10


BETA_ONE = 0.95
BETA_TWO = 0.95
EPSILON = 1e-08

MESH = pl.DeviceIdType.MESH
BF = jnp.bfloat16
F32 = jnp.float32


def send(src, dst, send_sem, recv_sem, where):
    return pltpu.make_async_remote_copy(
        src_ref=src,
        dst_ref=dst,
        send_sem=send_sem,
        recv_sem=recv_sem,
        device_id=where,
        device_id_type=MESH,
    )


def kernel(
    owners,
    subs,
    table,
    grad,
    left_hbm,
    right_hbm,
    one_hbm,
    two_hbm,
    update,
    one_out,
    two_out,
    left,
    left_t,
    right,
    one,
    two,
    one_new,
    two_new,
    grad_own,
    grad_far,
    grad_send,
    grad_recv,
    late_send,
    late_recv,
    far_send,
    far,
    part_send,
    part_recv,
    part_own,
    rot_send,
    rot_recv,
    rot_own,
    normed,
    back_sum,
    back,
    step_send,
    step_recv,
    load_sem,
    store_sem,
    gs_sem,
    gr_sem,
    as_sem,
    ar_sem,
    ls_sem,
    lr_sem,
    cs_sem,
    fs_sem,
    fr_sem,
    hs_sem,
    hr_sem,
    ps_sem,
    pr_sem,
    rs_sem,
    rr_sem,
    ns_sem,
    nr_sem,
    bs_sem,
    br_sem,
    us_sem,
    ur_sem,
):
    blocks, shard, share = grad.shape
    slots, half, order = left.shape
    tile = min(256, share)
    z = lax.axis_index("fsdp")
    x = lax.axis_index("sub")
    c = lax.axis_index("pair")
    z_peers = [lax.rem(z + d, owners) for d in range(1, owners)]
    x_peers = [lax.rem(x + d, subs) for d in range(1, subs)]

    loads = [
        pltpu.make_async_copy(src, dst, load_sem.at[n])
        for n, (src, dst) in enumerate(
            ((right_hbm, right), (left_hbm, left), (one_hbm, one), (two_hbm, two))
        )
    ]
    for load in loads:
        load.start()

    barrier = pltpu.get_barrier_semaphore()
    for o in z_peers:
        pl.semaphore_signal(barrier, inc=1, device_id={"fsdp": o}, device_id_type=MESH)
    for s in x_peers:
        pl.semaphore_signal(barrier, inc=1, device_id={"sub": s}, device_id_type=MESH)
    pl.semaphore_signal(barrier, inc=1, device_id={"pair": 1 - c}, device_id_type=MESH)

    owner = [table[b] for b in range(blocks)]
    rank = []
    for b in range(blocks):
        r = jnp.int32(0)
        for e in range(b):
            r = r + jnp.where(owner[e] == owner[b], 1, 0)
        rank.append(r)

    def source(o, k):
        n = jnp.int32(0)
        for b in range(blocks):
            n = n + jnp.where((owner[b] == o) & (rank[b] == k), b, 0)
        return n

    count = jnp.int32(0)
    for b in range(blocks):
        count = count + jnp.where(owner[b] == z, 1, 0)

    last = slots - 1
    chunks = share // tile
    part = share // 2
    other = pl.ds(pl.multiple_of((1 - c) * half, half), half)
    mine = pl.ds(pl.multiple_of(c * half, half), half)
    pending = []

    def go(src, dst, send_sem, recv_sem, where):
        copy = send(src, dst, send_sem, recv_sem, where)
        copy.start()
        pending.append(copy)
        return copy

    def arrive(ref, sem, where):
        send(ref, ref, sem, sem, where).wait_recv()

    grad_own[...] = grad[...].astype(BF)
    pl.semaphore_wait(barrier, len(z_peers) + len(x_peers) + 1)
    early = []
    for k in range(last):
        for d, o in enumerate(z_peers):
            grad_send[k, d] = grad_own[source(o, k)]
            copy = send(
                grad_send.at[k, d], grad_recv.at[k, z], gs_sem.at[k, d], gr_sem.at[k, z], {"fsdp": o}
            )
            copy.start()
            early.append(copy)
        grad_recv[k, z] = grad_own[source(z, k)]
    single = blocks < 2 * slots

    def travel(t, way):
        origin, after = z - way * t, z + way
        here = (origin >= 0) & (origin < owners)
        further = here & (after >= 0) & (after < owners)
        return here, further, jnp.clip(origin, 0, owners - 1), jnp.clip(after, 0, owners - 1)

    def chain(n, t, way, origin, after):
        return send(
            late_recv.at[n, origin],
            late_recv.at[n, origin],
            cs_sem.at[n, t, (1 - way) // 2],
            lr_sem.at[n, origin],
            {"fsdp": after},
        )

    def hop(n, t):
        for way in (1, -1):
            here, further, origin, after = travel(t, way)
            if t > 0:

                @pl.when(here)
                def _():
                    arrive(late_recv.at[n, origin], lr_sem.at[n, origin], {"fsdp": origin})

            if t < owners - 1:

                @pl.when(further)
                def _():
                    chain(n, t, way, origin, after).start()

    if single:
        only = jnp.int32(0)
        for b in range(blocks):
            only = only + jnp.where(rank[b] == last, b, 0)
        late_recv[0, z] = grad_own[jnp.minimum(only, blocks - 1)]
        for d, s in enumerate(x_peers):
            n = subs - 1 - d
            go(late_recv.at[0, z], late_recv.at[n, z], as_sem.at[d], ar_sem.at[n], {"sub": s})
        hop(0, 0)
    else:
        for d, s in enumerate(x_peers):
            go(grad_own, grad_far.at[x], as_sem.at[d], ar_sem.at[x], {"sub": s})

    def columns(s, n):
        return pl.ds(pl.multiple_of(s * share + n, tile), tile)

    def columns_of(s):
        return pl.ds(pl.multiple_of(s * share, share), share)

    loads[0].wait()
    for d, s in enumerate(x_peers):
        far_send[d] = right[last, pl.ds(pl.multiple_of(c * part, part), part), columns_of(s)]
        go(far_send.at[d], far.at[x, c], fs_sem.at[d], fr_sem.at[x], {"sub": s})

    loads[1].wait()
    for k in range(slots):
        for n in range(0, half, tile):
            left_t[k, :, n : n + tile] = left[k, n : n + tile, :].T

    if single:
        for n in range(1, subs):
            arrive(late_recv.at[n, z], ar_sem.at[n], {"sub": x_peers[n - 1]})
            hop(n, 0)
    else:
        for n, s in enumerate([x] + x_peers):
            if n == 1:
                for p in x_peers:
                    arrive(grad_far.at[p], ar_sem.at[p], {"sub": p})
            rows = (lambda i: grad_far[s, i]) if n else (lambda i: grad_own[i])
            for d, o in enumerate(z_peers):
                late_send[n, d] = rows(source(o, last))
                go(
                    late_send.at[n, d],
                    late_recv.at[n, z],
                    ls_sem.at[n, d],
                    lr_sem.at[n, z],
                    {"fsdp": o},
                )
            late_recv[n, z] = rows(source(z, last))
    for d, s in enumerate(x_peers):
        arrive(far.at[s, c], fr_sem.at[s], {"sub": s})
        go(far.at[s, c], far.at[s, c], hs_sem.at[d], hr_sem.at[d], {"pair": 1 - c})

    def rotate_right(k):
        for p in z_peers:
            arrive(grad_recv.at[k, p], gr_sem.at[k, p], {"fsdp": p})
        g = grad_recv[k].reshape(half, share)
        for ch in range(chunks):
            for d, s in enumerate(x_peers):
                part_send[k, d, ch] = jnp.dot(
                    g, right[k, :, columns(s, ch * tile)], preferred_element_type=F32
                ).astype(BF)
                go(
                    part_send.at[k, d, ch],
                    part_recv.at[k, x, ch],
                    ps_sem.at[k, d, ch],
                    pr_sem.at[k, x, ch],
                    {"sub": s},
                )
        for ch in range(chunks):
            part_own[k, ch] = jnp.dot(
                g, right[k, :, columns(x, ch * tile)], preferred_element_type=F32
            ).astype(BF)

    def collect(k, ch):
        total = part_own[k, ch].astype(F32)
        for s in x_peers:
            arrive(part_recv.at[k, s, ch], pr_sem.at[k, s, ch], {"sub": s})
            total = total + part_recv[k, s, ch].astype(F32)
        part_own[k, ch] = total.astype(BF)

    def rotate_right_last():
        for n in range(subs):
            if single:
                hop(n, owners - 1)
                continue
            for p in z_peers:
                arrive(late_recv.at[n, p], lr_sem.at[n, p], {"fsdp": p})
        for d, s in enumerate(x_peers):
            arrive(far.at[s, 1 - c], hr_sem.at[d], {"pair": 1 - c})
        for ch in range(chunks):
            total = jnp.dot(
                late_recv[0].reshape(half, share),
                right[last, :, columns(x, ch * tile)],
                preferred_element_type=F32,
            )
            for n, s in enumerate(x_peers):
                total = total + jnp.dot(
                    late_recv[n + 1].reshape(half, share),
                    far[s].reshape(share, share)[:, ch * tile : (ch + 1) * tile],
                    preferred_element_type=F32,
                )
            part_own[last, ch] = total.astype(BF)

    def rotate_left(k, ch):
        rot_send[k, ch] = jnp.dot(
            left_t[k, other, :], part_own[k, ch], preferred_element_type=F32
        ).astype(BF)
        go(
            rot_send.at[k, ch],
            rot_recv.at[k, ch],
            rs_sem.at[k, ch],
            rr_sem.at[k, ch],
            {"pair": 1 - c},
        )
        rot_own[...] = jnp.dot(left_t[k, mine, :], part_own[k, ch], preferred_element_type=F32)
        arrive(rot_recv.at[k, ch], rr_sem.at[k, ch], {"pair": 1 - c})

    corr_one = 1.0 - BETA_ONE**STEP
    corr_two = 1.0 - BETA_TWO**STEP

    def moments(k, ch):
        used = count > k
        rows = 64
        cols = slice(ch * tile, (ch + 1) * tile)

        @pl.loop(0, half // rows)
        def _(i):
            at = pl.ds(pl.multiple_of(i * rows, rows), rows)
            r = rot_own[at, :] + rot_recv[k, ch, at, :].astype(F32)
            m_old = one[at, k, cols]
            v_old = two[at, k, cols]
            m = BETA_ONE * m_old + (1.0 - BETA_ONE) * r
            v = BETA_TWO * v_old + (1.0 - BETA_TWO) * r * r
            one_new[at, k, cols] = jnp.where(used, m, m_old)
            two_new[at, k, cols] = jnp.where(used, v, v_old)
            normed[k, x, ch, at, :] = (
                m * (1.0 / corr_one) / (jnp.sqrt(v * (1.0 / corr_two)) + EPSILON)
            ).astype(BF)

        for d, s in enumerate(x_peers):
            go(
                normed.at[k, x, ch],
                normed.at[k, x, ch],
                ns_sem.at[k, d, ch],
                nr_sem.at[k, x, ch],
                {"sub": s},
            )

    def back_term(k, s, ch, n):
        return lax.dot_general(
            normed[k, s, ch],
            right[k, n * tile : (n + 1) * tile, columns(s, ch * tile)],
            (((1,), (1,)), ((), ())),
            preferred_element_type=F32,
        )

    def back_own(k):
        for n in range(chunks):
            total = back_term(k, x, 0, n)
            for ch in range(1, chunks):
                total = total + back_term(k, x, ch, n)
            back_sum[k, n] = total

    def back_rotate(k):
        for ch in range(chunks):
            for s in x_peers:
                arrive(normed.at[k, s, ch], nr_sem.at[k, s, ch], {"sub": s})
            for n in range(chunks):
                total = back_sum[k, n]
                for s in x_peers:
                    total = total + back_term(k, s, ch, n)
                if ch < chunks - 1:
                    back_sum[k, n] = total
                    continue
                back[k, n, c] = total.astype(BF)
                go(
                    back.at[k, n, c],
                    back.at[k, n, c],
                    bs_sem.at[k, n],
                    br_sem.at[k, n],
                    {"pair": 1 - c},
                )
        for n in range(chunks):
            arrive(back.at[k, n, 1 - c], br_sem.at[k, n], {"pair": 1 - c})
            step_send[k, n] = (
                jnp.dot(left[k], back[k, n].reshape(order, tile), preferred_element_type=F32)
                .astype(BF)
                .reshape(owners, shard, tile)
            )
            for d, o in enumerate(z_peers):
                go(
                    step_send.at[k, n, o],
                    step_recv.at[k, n, z],
                    us_sem.at[k, n, d],
                    ur_sem.at[k, n, z],
                    {"fsdp": o},
                )
            step_recv[k, n, z] = step_send[k, n, z]

    for k in range(last):
        rotate_right(k)
    if single and owners > 2:
        for n in range(subs):
            hop(n, 1)
    loads[2].wait()
    loads[3].wait()
    for k in range(last):
        for ch in range(chunks):
            collect(k, ch)
            rotate_left(k, ch)
            moments(k, ch)
            if single and k == 0 and ch == 0:
                for t in range(2, owners - 1):
                    for n in range(subs):
                        hop(n, t)
    rotate_right_last()
    for ch in range(chunks):
        rotate_left(last, ch)
        moments(last, ch)
    stores = [
        pltpu.make_async_copy(one_new, one_out, store_sem.at[0]),
        pltpu.make_async_copy(two_new, two_out, store_sem.at[1]),
    ]
    for store in stores:
        store.start()
    for k in range(last):
        back_own(k)
        back_rotate(k)
    back_own(last)
    back_rotate(last)
    for k in range(slots):
        for n in range(chunks):
            for p in z_peers:
                arrive(step_recv.at[k, n, p], ur_sem.at[k, n, p], {"fsdp": p})
    for n in range(chunks):
        for b in range(blocks):
            update[b, :, n * tile : (n + 1) * tile] = step_recv[
                jnp.minimum(rank[b], last), n, owner[b]
            ].astype(F32)
    for copy in early + pending:
        copy.wait_send()
    if single:
        for n in range(subs):
            for t in range(owners - 1):
                for way in (1, -1):
                    _, further, origin, after = travel(t, way)

                    @pl.when(further)
                    def _():
                        chain(n, t, way, origin, after).wait_send()

    for store in stores:
        store.wait()


def shards(
    owners, subs, gradient, owner_table, left_basis, right_basis, first_moment, second_moment
):
    slots, order = right_basis.shape[1], right_basis.shape[3]
    blocks, shard, share = gradient.shape
    half = owners * shard
    left_rows = left_basis.reshape(slots, half, order)
    right_rows = right_basis.reshape(slots, share, order)
    one = first_moment.reshape(half, slots, share)
    two = second_moment.reshape(half, slots, share)
    tile = min(256, share)
    chunks = share // tile
    dma = pltpu.SemaphoreType.DMA
    whole = pl.BlockSpec(memory_space=pl.ANY)
    vmem = pl.BlockSpec(memory_space=pltpu.VMEM)
    moment = jax.ShapeDtypeStruct((half, slots, share), F32)
    update, new_one, new_two = pl.pallas_call(
        functools.partial(kernel, owners, subs),
        out_shape=(jax.ShapeDtypeStruct((blocks, shard, share), F32), moment, moment),
        in_specs=[pl.BlockSpec(memory_space=pltpu.SMEM), vmem, whole, whole, whole, whole],
        out_specs=(vmem, whole, whole),
        scratch_shapes=[
            pltpu.VMEM((slots, half, order), BF),
            pltpu.VMEM((slots, order, half), BF),
            pltpu.VMEM((slots, share, order), BF),
            pltpu.VMEM((half, slots, share), F32),
            pltpu.VMEM((half, slots, share), F32),
            pltpu.VMEM((half, slots, share), F32),
            pltpu.VMEM((half, slots, share), F32),
            pltpu.VMEM((blocks, shard, share), BF),
            pltpu.VMEM((subs, blocks, shard, share), BF),
            pltpu.VMEM((slots - 1, owners - 1, shard, share), BF),
            pltpu.VMEM((slots - 1, owners, shard, share), BF),
            pltpu.VMEM((subs, owners - 1, shard, share), BF),
            pltpu.VMEM((subs, owners, shard, share), BF),
            pltpu.VMEM((subs - 1, share // 2, share), BF),
            pltpu.VMEM((subs, 2, share // 2, share), BF),
            pltpu.VMEM((slots - 1, subs - 1, chunks, half, tile), BF),
            pltpu.VMEM((slots - 1, subs, chunks, half, tile), BF),
            pltpu.VMEM((slots, chunks, half, tile), BF),
            pltpu.VMEM((slots, chunks, half, tile), BF),
            pltpu.VMEM((slots, chunks, half, tile), BF),
            pltpu.VMEM((half, tile), F32),
            pltpu.VMEM((slots, subs, chunks, half, tile), BF),
            pltpu.VMEM((slots, chunks, half, tile), F32),
            pltpu.VMEM((slots, chunks, 2, half, tile), BF),
            pltpu.VMEM((slots, chunks, owners, shard, tile), BF),
            pltpu.VMEM((slots, chunks, owners, shard, tile), BF),
            dma((4,)),
            dma((2,)),
            dma((slots, owners)),
            dma((slots, owners)),
            dma((subs,)),
            dma((subs,)),
            dma((subs, owners)),
            dma((subs, owners)),
            dma((subs, owners, 2)),
            dma((subs,)),
            dma((subs,)),
            dma((subs,)),
            dma((subs,)),
            dma((slots, subs, chunks)),
            dma((slots, subs, chunks)),
            dma((slots, chunks)),
            dma((slots, chunks)),
            dma((slots, subs, chunks)),
            dma((slots, subs, chunks)),
            dma((slots, chunks)),
            dma((slots, chunks)),
            dma((slots, chunks, owners)),
            dma((slots, chunks, owners)),
        ],
        compiler_params=pltpu.CompilerParams(
            collective_id=0, has_side_effects=True, vmem_limit_bytes=48 * 2**20
        ),
        cost_estimate=pl.CostEstimate(
            flops=10 * slots * half * order * share,
            bytes_accessed=20 * slots * half * share,
            transcendentals=slots * half * share,
        ),
    )(owner_table, gradient, left_rows, right_rows, one, two)
    return (update, new_one[None], new_two[None])


def solution(mesh):
    return jax.shard_map(
        functools.partial(shards, mesh.shape["fsdp"], mesh.shape["sub"]),
        mesh=mesh,
        in_specs=(
            P("groups", ("fsdp", "pair"), "sub"),
            P("groups"),
            P(("groups", "fsdp"), None, None, "pair", None, None),
            P(("groups", "fsdp"), None, "sub", None),
            P(("groups", "fsdp"), "pair", None, "sub"),
            P(("groups", "fsdp"), "pair", None, "sub"),
        ),
        out_specs=(
            P("groups", ("fsdp", "pair"), "sub"),
            P(("groups", "fsdp"), "pair", None, "sub"),
            P(("groups", "fsdp"), "pair", None, "sub"),
        ),
        check_vma=False,
    )
```
